32 devices in a mesh: lat: 4 (over x, core), lon: 4 (over z), lev: 2 (over y).
Axes of the slice: x: 2, y: 2, z: 4, core: 2. Of those that a mesh axis runs over, the one named last changes fastest.
Arguments:
- gradient: float32 [132, 128, 1536], P('lev', 'lat', 'lon'), may hold values from -6 to 6
- vertical: float32 [132, 132], replicated, may hold values from -0.5 to 0.5
- variance: float32 [132, 128, 1536], P('lev', 'lat', 'lon'), may hold values from 0.25 to 4
Outputs:
- increment: float32 [132, 128, 1536], P('lev', 'lat', 'lon')
The draws below stay inside these ranges and needn't reach their ends.
All inputs are finite; a program needn't handle non-finite values.
Results may differ from the reference program's by a relative error of at most 0.000078.
Values sent between devices are 32-bit elements; how exact they have to be, the bound alone decides.
A program may use at most 64 MiB of HBM per device.

```python
import math
import jax
import jax.numpy as jnp
from jax import lax

LEV = 132
HALO = 32
LAT = 128
LON = 1536


def block_scale(own_key, extent, pieces, least, largest):
    def one(position, shards_of):
        heights = jax.random.uniform(jax.random.fold_in(jax.random.fold_in(own_key, 6), position), (shards_of,), jnp.float32, least / len(pieces), largest / len(pieces))
        return jnp.repeat(jnp.exp(heights), extent[position] // shards_of).reshape((-1,) + (1,) * (len(extent) - position - 1))

    gain = one(*pieces[0])
    for cut in pieces[1:]:
        gain = gain * one(*cut)
    return gain


def centred(key, dims, scale, limit, cuts=(), kind=jnp.bfloat16):
    level = block_scale(key, dims, cuts, -0.22, 0.18) if cuts else 1.0
    drawn = jax.random.normal(key, dims, jnp.float32) * scale * level
    return jnp.minimum(jnp.maximum(drawn, -limit), limit).astype(kind)


def setup_inputs(seed: int = 0) -> dict:
    arg_keys = jax.random.split(jax.random.key(seed), 4)
    return {
        "gradient": centred(arg_keys[0], (LEV, LAT, LON), 1.0, 6.0, ((0, 2), (1, 4), (2, 4)), jnp.float32),
        "vertical": centred(arg_keys[1], (LEV, LEV), LEV ** -0.5, 0.5, (), jnp.float32),
        "variance": jnp.clip(jnp.exp(math.log(4.0) - 2.7725887 * jax.random.uniform(arg_keys[2], (LEV, LAT, LON), jnp.float32) ** block_scale(arg_keys[2], (LEV, LAT, LON), ((0, 2), (1, 4), (2, 4)), -0.2, 0.2)), 0.25, 4.0),
    }


def kernel_weights():
    offsets = jnp.arange(-HALO, HALO + 1).astype(jnp.float32)
    bell = jnp.exp(-0.5 * (2.0 * offsets / HALO) ** 2)
    return bell / (jnp.sqrt(jnp.sum(bell)) * jnp.sqrt(jnp.sqrt(jnp.sum(bell * bell))))

def filter_lat(field, weights):
    padded = jnp.pad(field, ((0, 0), (HALO, HALO), (0, 0)))
    rows = field.shape[1]
    total = jnp.zeros_like(field)
    for step in range(2 * HALO + 1):
        total = total + weights[step] * padded[:, step:step + rows, :]
    return total

def filter_lon(field, weights):
    padded = jnp.concatenate([field[:, :, -HALO:], field, field[:, :, :HALO]], axis=2)
    cols = field.shape[2]
    total = jnp.zeros_like(field)
    for step in range(2 * HALO + 1):
        total = total + weights[step] * padded[:, :, step:step + cols]
    return total

def reference(gradient, vertical, variance):
    weights = kernel_weights()
    shape = gradient.shape
    columns = jnp.dot(vertical, gradient.reshape(shape[0], -1), precision=lax.Precision.HIGHEST).reshape(shape)
    smooth = filter_lon(filter_lat(columns, weights), weights)
    scaled = variance * smooth
    return filter_lat(filter_lon(scaled, weights), weights)
```

```python
import functools
import math

import jax
import jax.numpy as jnp
import ml_dtypes
import numpy as np
from jax import lax
from jax.experimental import pallas as pl
from jax.experimental.pallas import tpu as pltpu
from jax.sharding import PartitionSpec as P

HALO = 32
MAX_CHUNKS = 11
AHEAD = 2
LANES = 128
MESH = pl.DeviceIdType.MESH


def taps(offset):
    steps = np.arange(-HALO, HALO + 1, dtype=np.float64)
    bell = np.exp(-0.5 * (2.0 * steps / HALO) ** 2)
    scale = 1.0 / (math.sqrt(bell.sum()) * math.sqrt(math.sqrt((bell * bell).sum())))
    values = np.exp(-0.5 * (2.0 * offset / HALO) ** 2) * scale
    return np.where(np.abs(offset) <= HALO, values, 0.0).astype(np.float32)


def parts_np(values):
    high = values.astype(ml_dtypes.bfloat16)
    low = (values - high.astype(np.float32)).astype(ml_dtypes.bfloat16)
    return high, low


def lat_matrix(rows):
    place = np.arange(-HALO, rows + HALO)
    high, low = parts_np(taps((place[None, :] - np.arange(rows)[:, None]).astype(np.float64)))
    return np.concatenate(
        [np.concatenate([high, high], 1), np.concatenate([low, np.zeros_like(low)], 1)], 0
    )


def lon_matrices(cols):
    place = np.concatenate([np.arange(cols), np.arange(-HALO, 0), np.arange(cols, cols + HALO)])
    values = taps((place[:, None] - np.arange(cols)[None, :]).astype(np.float64))
    values = np.pad(values, ((0, LANES - 2 * HALO), (0, 0)))
    return np.stack(parts_np(values))


def split(x):
    high = x.astype(jnp.bfloat16)
    return high, (x - high.astype(jnp.float32)).astype(jnp.bfloat16)


def dot(a, b):
    return jnp.dot(a, b, preferred_element_type=jnp.float32)


def kernel(
    sizes, g_hbm, v_ref, var_hbm, plat_ref, qlon_hbm, out_hbm,
    g, part, own, ry, col, hx1, pc, ez1, rz1, sc, ez2, rz2, q2, hx2, out, var, qlon,
    in_sem, ys, yr, x1s, x1r, z1s, z1r, z2s, z2r, x2s, x2r, out_sem,
):
    levels, rows, cols, n_lev, n_lat, n_lon, chunks, padded = sizes
    each = levels // chunks
    span = each * rows
    groups = LANES // HALO
    band = rows // groups
    espan = each * band

    lev, lat, lon = lax.axis_index("lev"), lax.axis_index("lat"), lax.axis_index("lon")
    lon_next, lon_prev = lax.rem(lon + 1, n_lon), lax.rem(lon + n_lon - 1, n_lon)
    has_prev, has_next = lat > 0, lat < n_lat - 1

    tiles = cols // LANES
    loads_g = [
        pltpu.make_async_copy(
            g_hbm.at[:, pl.ds(c * LANES, LANES)], g.at[c, pl.ds(0, levels * rows)], in_sem.at[2 + c]
        )
        for c in range(tiles)
    ]
    load_q = pltpu.make_async_copy(qlon_hbm, qlon, in_sem.at[1])
    load_v = pltpu.make_async_copy(var_hbm, var, in_sem.at[0])
    for load in loads_g:
        load.start()
    load_q.start()
    load_v.start()

    barrier = pltpu.get_barrier_semaphore()

    def greet(target):
        pl.semaphore_signal(barrier, inc=1, device_id=target, device_id_type=MESH)

    for d in range(1, n_lev):
        greet({"lev": lax.rem(lev + d, n_lev)})
    greet({"lon": lon_next})
    greet({"lon": lon_prev})

    @pl.when(has_prev)
    def _():
        greet({"lat": lat - 1})

    @pl.when(has_next)
    def _():
        greet({"lat": lat + 1})

    peers = n_lev + 1 + jnp.minimum(lat, 1) + jnp.minimum(n_lat - 1 - lat, 1)
    pl.semaphore_wait(barrier, peers)

    if padded > levels:
        g[:, levels * rows:, :] = jnp.zeros((tiles, (padded - levels) * rows, LANES), jnp.float32)
    for load in loads_g:
        load.wait()

    def mixing(owner):
        block = jnp.zeros((levels, levels), jnp.float32)
        for a in range(n_lev):
            for b in range(n_lev):
                piece = v_ref[a * levels:(a + 1) * levels, b * levels:(b + 1) * levels]
                block = jnp.where(jnp.logical_and(owner == a, lev == b), piece, block)
        block = jnp.concatenate([block, jnp.zeros((levels, padded - levels), jnp.float32)], axis=1)
        high, low = split(block)
        return jnp.concatenate([high, low, high], axis=1)

    def mix(matrix, store):
        def body(r, carry):
            x = jnp.concatenate([g[c, pl.ds(r, padded, stride=rows), :] for c in range(tiles)], axis=1)
            high, low = split(x)
            store(r, dot(matrix, jnp.concatenate([high, high, low], axis=0)))
            return carry

        lax.fori_loop(0, rows, body, 0, unroll=2)

    def y_copy(d, k):
        at = pl.ds(pl.multiple_of(k * span, span), span)
        return pltpu.make_async_remote_copy(
            part.at[d - 1, :, at], ry.at[d - 1, :, at], ys.at[d - 1, k], yr.at[d - 1, k],
            device_id={"lev": lax.rem(lev + d, n_lev)}, device_id_type=MESH,
        )

    def x_copy(src, dst, send, recv, side, k):
        at = pl.ds(pl.multiple_of(k * span, span), span)
        return pltpu.make_async_remote_copy(
            src.at[at], dst.at[side, at], send.at[side, k], recv.at[side, k],
            device_id={"lat": jnp.clip(lat + (1 if side == 0 else -1), 0, n_lat - 1)}, device_id_type=MESH,
        )

    def z_copy(src, dst, send, recv, side, k):
        at = pl.ds(pl.multiple_of(k * espan, espan), espan)
        return pltpu.make_async_remote_copy(
            src.at[side, at], dst.at[side, at], send.at[side, k], recv.at[side, k],
            device_id={"lon": lon_next if side == 0 else lon_prev}, device_id_type=MESH,
        )

    def x_send(*a, k):
        @pl.when(has_next)
        def _():
            x_copy(*a, 0, k).start()

        @pl.when(has_prev)
        def _():
            x_copy(*a, 1, k).start()

    def x_recv(*a, k):
        @pl.when(has_prev)
        def _():
            x_copy(*a, 0, k).wait_recv()

        @pl.when(has_next)
        def _():
            x_copy(*a, 1, k).wait_recv()

    lane = lax.broadcasted_iota(jnp.int32, (espan, LANES), 1)

    def pack(tile, base):
        tile = tile.reshape(each, groups, band, LANES)
        packed = None
        for q in range(groups):
            shift = (HALO * q - base) % LANES
            moved = tile[:, q].reshape(espan, LANES)
            moved = pltpu.roll(moved, shift, 1) if shift else moved
            packed = moved if packed is None else jnp.where(lane >= HALO * q, moved, packed)
        return packed

    def unpack(left, right):
        out_rows = []
        for q in range(groups):
            a, b = (-HALO * q) % LANES, (HALO - HALO * q) % LANES
            moved_l = pltpu.roll(left, a, 1) if a else left
            moved_r = pltpu.roll(right, b, 1) if b else right
            out_rows.append(jnp.where(lane < HALO, moved_l, moved_r).reshape(each, 1, band, LANES))
        return jnp.concatenate(out_rows, axis=1).reshape(span, LANES)

    def along_lat(before, here, after):
        blocks = jnp.concatenate(
            [
                jnp.concatenate([x[i * rows:(i + 1) * rows] for i in range(each)], axis=1)
                for x in (before, here, after)
            ],
            axis=0,
        )
        high, low = split(blocks)
        both = dot(plat_ref[...], jnp.concatenate([high, low], axis=0))
        both = both[:rows] + both[rows:]
        return jnp.concatenate([both[:, i * cols:(i + 1) * cols] for i in range(each)], axis=0)

    def along_lon(here, left, right):
        high, low = split(jnp.concatenate([here, unpack(left, right)], axis=1))
        return dot(high, qlon[0]) + (dot(low, qlon[0]) + dot(high, qlon[1]))

    for d in range(1, n_lev):
        def store(r, value, d=d):
            for c in range(tiles):
                part[d - 1, c, pl.ds(r, levels, stride=rows), :] = value[:, c * LANES:(c + 1) * LANES]

        mix(mixing(lax.rem(lev + d, n_lev)), store)
    for k in range(min(AHEAD, chunks)):
        for d in range(1, n_lev):
            y_copy(d, k).start()

    def store_own(r, value):
        for c in range(tiles):
            own[c, pl.ds(r, levels, stride=rows), :] = value[:, c * LANES:(c + 1) * LANES]

    mix(mixing(lev), store_own)

    @pl.when(jnp.logical_not(has_prev))
    def _():
        hx1[0] = jnp.zeros((levels * rows, cols), jnp.float32)
        hx2[0] = jnp.zeros((levels * rows, cols), jnp.float32)

    @pl.when(jnp.logical_not(has_next))
    def _():
        hx1[1] = jnp.zeros((levels * rows, cols), jnp.float32)
        hx2[1] = jnp.zeros((levels * rows, cols), jnp.float32)

    load_q.wait()
    load_v.wait()

    x1 = (col, hx1, x1s, x1r)
    x2 = (q2, hx2, x2s, x2r)
    z1 = (ez1, rz1, z1s, z1r)
    z2 = (ez2, rz2, z2s, z2r)

    def out_copy(k):
        at = pl.ds(pl.multiple_of(k * span, span), span)
        return pltpu.make_async_copy(out.at[at], out_hbm.at[at], out_sem.at[k])

    def z_send(value, edges, args, k):
        eat = pl.ds(pl.multiple_of(k * espan, espan), espan)
        edges[0, eat] = pack(value[:, cols - LANES:], LANES - HALO)
        edges[1, eat] = pack(value[:, :LANES], 0)
        z_copy(*args, 0, k).start()
        z_copy(*args, 1, k).start()

    def z_recv(recv, args, k):
        z_copy(*args, 0, k).wait_recv()
        z_copy(*args, 1, k).wait_recv()
        eat = pl.ds(pl.multiple_of(k * espan, espan), espan)
        return recv[0, eat], recv[1, eat]

    def step(t, carry):
        def stage(lag, body):
            k = t - lag

            @pl.when(jnp.logical_and(k >= 0, k < chunks))
            def _():
                body(k, pl.ds(pl.multiple_of(k * span, span), span))

        def stage_send(k, at):
            for d in range(1, n_lev):
                y_copy(d, k).start()

        def stage_mix(k, at):
            total = own[:, at]
            for d in range(1, n_lev):
                y_copy(d, k).wait_recv()
                total = total + ry[d - 1, :, at]
            for c in range(tiles):
                col[at, c * LANES:(c + 1) * LANES] = total[c]
            x_send(*x1, k=k)

        def stage_p1(k, at):
            x_recv(*x1, k=k)
            value = along_lat(hx1[0, at], col[at], hx1[1, at])
            pc[at] = value
            z_send(value, ez1, z1, k)

        def stage_q1(k, at):
            left, right = z_recv(rz1, z1, k)
            value = var[at] * along_lon(pc[at], left, right)
            sc[at] = value
            z_send(value, ez2, z2, k)

        def stage_q2(k, at):
            left, right = z_recv(rz2, z2, k)
            q2[at] = along_lon(sc[at], left, right)
            x_send(*x2, k=k)

        def stage_p2(k, at):
            x_recv(*x2, k=k)
            out[at] = along_lat(hx2[0, at], q2[at], hx2[1, at])
            out_copy(k).start()

        stage(-AHEAD, stage_send)
        stage(0, stage_mix)
        stage(1, stage_p1)
        stage(2, stage_q1)
        stage(3, stage_q2)
        stage(4, stage_p2)
        return carry

    lax.fori_loop(0, chunks + 4, step, 0)

    def drain(k, carry):
        for d in range(1, n_lev):
            y_copy(d, k).wait_send()
        for args in (z1, z2):
            z_copy(*args, 0, k).wait_send()
            z_copy(*args, 1, k).wait_send()

        @pl.when(has_next)
        def _():
            x_copy(*x1, 0, k).wait_send()
            x_copy(*x2, 0, k).wait_send()

        @pl.when(has_prev)
        def _():
            x_copy(*x1, 1, k).wait_send()
            x_copy(*x2, 1, k).wait_send()

        out_copy(k).wait()
        return carry

    lax.fori_loop(0, chunks, drain, 0)


def on_device(gradient, vertical, variance):
    levels, rows, cols = gradient.shape
    n_lev, n_lat, n_lon = (lax.axis_size(a) for a in ("lev", "lat", "lon"))
    chunks = max(c for c in range(1, MAX_CHUNKS + 1) if levels % c == 0)
    padded = -(-levels // 16) * 16
    band = rows * HALO // LANES
    sizes = (levels, rows, cols, n_lev, n_lat, n_lon, chunks, padded)
    plane = levels * rows
    f32 = jnp.float32
    dma = pltpu.SemaphoreType.DMA
    qlon = lon_matrices(cols)
    plat = lat_matrix(rows)
    anywhere = pl.BlockSpec(memory_space=pl.ANY)
    vmem = pl.BlockSpec(memory_space=pltpu.VMEM)
    full = pltpu.VMEM((plane, cols), f32)
    tiles = cols // LANES
    others = pltpu.VMEM((n_lev - 1, tiles, plane, LANES), f32)
    own = pltpu.VMEM((tiles, plane, LANES), f32)
    sides = pltpu.VMEM((2, plane, cols), f32)
    edges = pltpu.VMEM((2, levels * band, LANES), f32)
    pair = dma((2, chunks))
    result = pl.pallas_call(
        functools.partial(kernel, sizes),
        out_shape=jax.ShapeDtypeStruct((plane, cols), f32),
        in_specs=[anywhere, vmem, anywhere, vmem, anywhere],
        out_specs=anywhere,
        scratch_shapes=[
            pltpu.VMEM((tiles, padded * rows, LANES), f32),
            others, own, others, full, sides, full, edges, edges, full, edges, edges, full, sides, full, full,
            pltpu.VMEM(qlon.shape, jnp.bfloat16),
            dma((2 + tiles,)), dma((n_lev - 1, chunks)), dma((n_lev - 1, chunks)),
            pair, pair, pair, pair, pair, pair, pair, pair, dma((chunks,)),
        ],
        compiler_params=pltpu.CompilerParams(
            collective_id=0, has_side_effects=True, vmem_limit_bytes=60 * 1024 * 1024
        ),
    )(
        gradient.reshape(plane, cols), vertical, variance.reshape(plane, cols),
        jnp.asarray(plat), jnp.asarray(qlon),
    )
    return result.reshape(levels, rows, cols)


def solution(mesh):
    return jax.shard_map(
        on_device,
        mesh=mesh,
        in_specs=(P("lev", "lat", "lon"), P(), P("lev", "lat", "lon")),
        out_specs=P("lev", "lat", "lon"),
        check_vma=False,
    )
```

```python
import functools
import math

import jax
import jax.numpy as jnp
import ml_dtypes
import numpy as np
from jax import lax
from jax.experimental import pallas as pl
from jax.experimental.pallas import tpu as pltpu
from jax.sharding import PartitionSpec as P

HALO = 32
MAX_CHUNKS = 11
AHEAD = 4
LANES = 128
MESH = pl.DeviceIdType.MESH


def taps(offset):
    steps = np.arange(-HALO, HALO + 1, dtype=np.float64)
    bell = np.exp(-0.5 * (2.0 * steps / HALO) ** 2)
    scale = 1.0 / (math.sqrt(bell.sum()) * math.sqrt(math.sqrt((bell * bell).sum())))
    values = np.exp(-0.5 * (2.0 * offset / HALO) ** 2) * scale
    return np.where(np.abs(offset) <= HALO, values, 0.0).astype(np.float32)


def parts_np(values):
    high = values.astype(ml_dtypes.bfloat16)
    low = (values - high.astype(np.float32)).astype(ml_dtypes.bfloat16)
    return high, low


def lat_matrix(rows):
    place = np.arange(-HALO, rows + HALO)
    high, low = parts_np(taps((place[None, :] - np.arange(rows)[:, None]).astype(np.float64)))
    return np.concatenate(
        [np.concatenate([high, high], 1), np.concatenate([low, np.zeros_like(low)], 1)], 0
    )


def lon_matrices(cols):
    place = np.concatenate([np.arange(cols), np.arange(-HALO, 0), np.arange(cols, cols + HALO)])
    values = taps((place[:, None] - np.arange(cols)[None, :]).astype(np.float64))
    values = np.pad(values, ((0, LANES - 2 * HALO), (0, 0)))
    return np.stack(parts_np(values))


def split(x):
    high = x.astype(jnp.bfloat16)
    return high, (x - high.astype(jnp.float32)).astype(jnp.bfloat16)


def dot(a, b):
    return jnp.dot(a, b, preferred_element_type=jnp.float32)


def kernel(
    sizes, g_hbm, v_ref, var_hbm, plat_ref, qlon_hbm, out_hbm,
    g, hg, pg, part, own, ry, col, hx1, pc, ez1, rz1, sc, ez2, rz2, q2, hx2, out, var, qlon,
    in_sem, xgs, xgr, ys, yr, x1s, x1r, z1s, z1r, z2s, z2r, x2s, x2r, out_sem,
):
    levels, rows, cols, n_lev, n_lat, n_lon, chunks, padded = sizes
    each = levels // chunks
    span = each * rows
    groups = LANES // HALO
    band = rows // groups
    espan = each * band

    lev, lat, lon = lax.axis_index("lev"), lax.axis_index("lat"), lax.axis_index("lon")
    lon_next, lon_prev = lax.rem(lon + 1, n_lon), lax.rem(lon + n_lon - 1, n_lon)
    has_prev, has_next = lat > 0, lat < n_lat - 1

    tiles = cols // LANES
    last = tiles - 1
    main = cols - LANES
    plane = levels * rows
    loads_g = [
        pltpu.make_async_copy(
            g_hbm.at[:, pl.ds(c * LANES, LANES)], g.at[c, pl.ds(0, levels * rows)], in_sem.at[2 + c]
        )
        for c in range(tiles)
    ]
    load_q = pltpu.make_async_copy(qlon_hbm, qlon, in_sem.at[1])
    load_v = pltpu.make_async_copy(var_hbm, var, in_sem.at[0])
    for load in loads_g[::-1]:
        load.start()
    load_q.start()
    load_v.start()

    barrier = pltpu.get_barrier_semaphore()

    def greet(target):
        pl.semaphore_signal(barrier, inc=1, device_id=target, device_id_type=MESH)

    for d in range(1, n_lev):
        greet({"lev": lax.rem(lev + d, n_lev)})
    greet({"lon": lon_next})
    greet({"lon": lon_prev})

    @pl.when(has_prev)
    def _():
        greet({"lat": lat - 1})

    @pl.when(has_next)
    def _():
        greet({"lat": lat + 1})

    peers = n_lev + 1 + jnp.minimum(lat, 1) + jnp.minimum(n_lat - 1 - lat, 1)
    pl.semaphore_wait(barrier, peers)

    loads_g[last].wait()

    def raw_copy(side):
        return pltpu.make_async_remote_copy(
            g.at[last, pl.ds(0, plane)], hg.at[side], xgs.at[side], xgr.at[side],
            device_id={"lat": jnp.clip(lat + (1 if side == 0 else -1), 0, n_lat - 1)}, device_id_type=MESH,
        )

    @pl.when(has_next)
    def _():
        raw_copy(0).start()

    @pl.when(has_prev)
    def _():
        raw_copy(1).start()

    if padded > levels:
        extra = (padded - levels) * rows
        g[:last, plane:, :] = jnp.zeros((last, extra, LANES), jnp.float32)
        pg[plane:, :] = jnp.zeros((extra, LANES), jnp.float32)
    for load in loads_g[:last]:
        load.wait()

    def mixing(owner):
        block = jnp.zeros((levels, levels), jnp.float32)
        for a in range(n_lev):
            for b in range(n_lev):
                piece = v_ref[a * levels:(a + 1) * levels, b * levels:(b + 1) * levels]
                block = jnp.where(jnp.logical_and(owner == a, lev == b), piece, block)
        block = jnp.concatenate([block, jnp.zeros((levels, padded - levels), jnp.float32)], axis=1)
        high, low = split(block)
        return jnp.concatenate([high, low, high], axis=1)

    def mix(matrix, wanted, store):
        def body(r, carry):
            at = pl.ds(r, padded, stride=rows)
            x = jnp.concatenate([pg[at, :] if c == last else g[c, at, :] for c in wanted], axis=1)
            high, low = split(x)
            value = dot(matrix, jnp.concatenate([high, high, low], axis=0))
            for i, c in enumerate(wanted):
                store(c, pl.ds(r, levels, stride=rows), value[:, i * LANES:(i + 1) * LANES])
            return carry

        lax.fori_loop(0, rows, body, 0, unroll=4)

    def mix_others(wanted):
        for d in range(1, n_lev):
            def store(c, at, value, d=d):
                part[d - 1, c, at, :] = value

            mix(mixing(lax.rem(lev + d, n_lev)), wanted, store)

    def mix_own(wanted):
        def store(c, at, value):
            own[c, at, :] = value

        mix(mixing(lev), wanted, store)

    def y_copy(d, k, late):
        at = pl.ds(pl.multiple_of(k * span, span), span)
        which = pl.ds(last, 1) if late else pl.ds(0, last)
        return pltpu.make_async_remote_copy(
            part.at[d - 1, which, at], ry.at[d - 1, which, at],
            ys.at[d - 1, 2 * k + late], yr.at[d - 1, 2 * k + late],
            device_id={"lev": lax.rem(lev + d, n_lev)}, device_id_type=MESH,
        )

    def x_copy(src, dst, send, recv, side, k):
        at = pl.ds(pl.multiple_of(k * span, span), span)
        return pltpu.make_async_remote_copy(
            src.at[at], dst.at[side, at], send.at[side, k], recv.at[side, k],
            device_id={"lat": jnp.clip(lat + (1 if side == 0 else -1), 0, n_lat - 1)}, device_id_type=MESH,
        )

    def z_copy(src, dst, send, recv, side, k):
        at = pl.ds(pl.multiple_of(k * espan, espan), espan)
        return pltpu.make_async_remote_copy(
            src.at[side, at], dst.at[side, at], send.at[side, k], recv.at[side, k],
            device_id={"lon": lon_next if side == 0 else lon_prev}, device_id_type=MESH,
        )

    def x_send(*a, k):
        @pl.when(has_next)
        def _():
            x_copy(*a, 0, k).start()

        @pl.when(has_prev)
        def _():
            x_copy(*a, 1, k).start()

    def x_recv(*a, k):
        @pl.when(has_prev)
        def _():
            x_copy(*a, 0, k).wait_recv()

        @pl.when(has_next)
        def _():
            x_copy(*a, 1, k).wait_recv()

    lane = lax.broadcasted_iota(jnp.int32, (espan, LANES), 1)

    def pack(tile, base):
        tile = tile.reshape(each, groups, band, LANES)
        packed = None
        for q in range(groups):
            shift = (HALO * q - base) % LANES
            moved = tile[:, q].reshape(espan, LANES)
            moved = pltpu.roll(moved, shift, 1) if shift else moved
            packed = moved if packed is None else jnp.where(lane >= HALO * q, moved, packed)
        return packed

    def unpack(left, right):
        out_rows = []
        for q in range(groups):
            a, b = (-HALO * q) % LANES, (HALO - HALO * q) % LANES
            moved_l = pltpu.roll(left, a, 1) if a else left
            moved_r = pltpu.roll(right, b, 1) if b else right
            out_rows.append(jnp.where(lane < HALO, moved_l, moved_r).reshape(each, 1, band, LANES))
        return jnp.concatenate(out_rows, axis=1).reshape(span, LANES)

    def along_lat(before, here, after):
        width = here.shape[1]
        blocks = jnp.concatenate(
            [
                jnp.concatenate([x[i * rows:(i + 1) * rows] for i in range(each)], axis=1)
                for x in (before, here, after)
            ],
            axis=0,
        )
        high, low = split(blocks)
        both = dot(plat_ref[...], jnp.concatenate([high, low], axis=0))
        both = both[:rows] + both[rows:]
        return jnp.concatenate([both[:, i * width:(i + 1) * width] for i in range(each)], axis=0)

    def along_lon(here, left, right):
        high, low = split(jnp.concatenate([here, unpack(left, right)], axis=1))
        return dot(high, qlon[0]) + (dot(low, qlon[0]) + dot(high, qlon[1]))

    mix_others(range(last))
    for k in range(min(AHEAD, chunks)):
        for d in range(1, n_lev):
            y_copy(d, k, 0).start()
    mix_own(range(last))

    @pl.when(jnp.logical_not(has_prev))
    def _():
        hx1[0] = jnp.zeros((plane, main), jnp.float32)
        hg[0] = jnp.zeros((plane, LANES), jnp.float32)
        hx2[0] = jnp.zeros((levels * rows, cols), jnp.float32)

    @pl.when(jnp.logical_not(has_next))
    def _():
        hx1[1] = jnp.zeros((plane, main), jnp.float32)
        hg[1] = jnp.zeros((plane, LANES), jnp.float32)
        hx2[1] = jnp.zeros((levels * rows, cols), jnp.float32)

    @pl.when(has_prev)
    def _():
        raw_copy(0).wait_recv()

    @pl.when(has_next)
    def _():
        raw_copy(1).wait_recv()

    def early(k, carry):
        at = pl.ds(pl.multiple_of(k * span, span), span)
        pg[at] = along_lat(hg[0, at], g[last, at], hg[1, at])
        return carry

    lax.fori_loop(0, chunks, early, 0)
    mix_others([last])
    for k in range(min(AHEAD, chunks)):
        for d in range(1, n_lev):
            y_copy(d, k, 1).start()
    mix_own([last])

    load_q.wait()
    load_v.wait()

    x1 = (col, hx1, x1s, x1r)
    x2 = (q2, hx2, x2s, x2r)
    z1 = (ez1, rz1, z1s, z1r)
    z2 = (ez2, rz2, z2s, z2r)

    def out_copy(k):
        at = pl.ds(pl.multiple_of(k * span, span), span)
        return pltpu.make_async_copy(out.at[at], out_hbm.at[at], out_sem.at[k])

    def z_send(value, edges, args, k):
        eat = pl.ds(pl.multiple_of(k * espan, espan), espan)
        edges[0, eat] = pack(value[:, cols - LANES:], LANES - HALO)
        edges[1, eat] = pack(value[:, :LANES], 0)
        z_copy(*args, 0, k).start()
        z_copy(*args, 1, k).start()

    def z_recv(recv, args, k):
        z_copy(*args, 0, k).wait_recv()
        z_copy(*args, 1, k).wait_recv()
        eat = pl.ds(pl.multiple_of(k * espan, espan), espan)
        return recv[0, eat], recv[1, eat]

    def step(t, carry):
        def stage(lag, body):
            k = t - lag

            @pl.when(jnp.logical_and(k >= 0, k < chunks))
            def _():
                body(k, pl.ds(pl.multiple_of(k * span, span), span))

        def stage_send(k, at):
            for late in (0, 1):
                for d in range(1, n_lev):
                    y_copy(d, k, late).start()

        def stage_mix(k, at):
            total = own[:last, at]
            for d in range(1, n_lev):
                y_copy(d, k, 0).wait_recv()
                total = total + ry[d - 1, :last, at]
            for c in range(last):
                col[at, c * LANES:(c + 1) * LANES] = total[c]
            x_send(*x1, k=k)

        def stage_p1(k, at):
            x_recv(*x1, k=k)
            total = own[last, at]
            for d in range(1, n_lev):
                y_copy(d, k, 1).wait_recv()
                total = total + ry[d - 1, last, at]
            value = jnp.concatenate([along_lat(hx1[0, at], col[at], hx1[1, at]), total], axis=1)
            pc[at] = value
            z_send(value, ez1, z1, k)

        def stage_q1(k, at):
            left, right = z_recv(rz1, z1, k)
            value = var[at] * along_lon(pc[at], left, right)
            sc[at] = value
            z_send(value, ez2, z2, k)

        def stage_q2(k, at):
            left, right = z_recv(rz2, z2, k)
            q2[at] = along_lon(sc[at], left, right)
            x_send(*x2, k=k)

        def stage_p2(k, at):
            x_recv(*x2, k=k)
            out[at] = along_lat(hx2[0, at], q2[at], hx2[1, at])
            out_copy(k).start()

        stage(-AHEAD, stage_send)
        stage(0, stage_mix)
        stage(1, stage_p1)
        stage(2, stage_q1)
        stage(3, stage_q2)
        stage(4, stage_p2)
        return carry

    lax.fori_loop(0, chunks + 4, step, 0)

    def drain(k, carry):
        for d in range(1, n_lev):
            y_copy(d, k, 0).wait_send()
            y_copy(d, k, 1).wait_send()
        for args in (z1, z2):
            z_copy(*args, 0, k).wait_send()
            z_copy(*args, 1, k).wait_send()

        @pl.when(has_next)
        def _():
            x_copy(*x1, 0, k).wait_send()
            x_copy(*x2, 0, k).wait_send()

        @pl.when(has_prev)
        def _():
            x_copy(*x1, 1, k).wait_send()
            x_copy(*x2, 1, k).wait_send()

        out_copy(k).wait()
        return carry

    lax.fori_loop(0, chunks, drain, 0)

    @pl.when(has_next)
    def _():
        raw_copy(0).wait_send()

    @pl.when(has_prev)
    def _():
        raw_copy(1).wait_send()


def on_device(gradient, vertical, variance):
    levels, rows, cols = gradient.shape
    n_lev, n_lat, n_lon = (lax.axis_size(a) for a in ("lev", "lat", "lon"))
    chunks = max(c for c in range(1, MAX_CHUNKS + 1) if levels % c == 0)
    padded = -(-levels // 16) * 16
    band = rows * HALO // LANES
    sizes = (levels, rows, cols, n_lev, n_lat, n_lon, chunks, padded)
    plane = levels * rows
    f32 = jnp.float32
    dma = pltpu.SemaphoreType.DMA
    qlon = lon_matrices(cols)
    plat = lat_matrix(rows)
    anywhere = pl.BlockSpec(memory_space=pl.ANY)
    vmem = pl.BlockSpec(memory_space=pltpu.VMEM)
    full = pltpu.VMEM((plane, cols), f32)
    tiles = cols // LANES
    others = pltpu.VMEM((n_lev - 1, tiles, plane, LANES), f32)
    own = pltpu.VMEM((tiles, plane, LANES), f32)
    sides = pltpu.VMEM((2, plane, cols), f32)
    edges = pltpu.VMEM((2, levels * band, LANES), f32)
    pair = dma((2, chunks))
    result = pl.pallas_call(
        functools.partial(kernel, sizes),
        out_shape=jax.ShapeDtypeStruct((plane, cols), f32),
        in_specs=[anywhere, vmem, anywhere, vmem, anywhere],
        out_specs=anywhere,
        scratch_shapes=[
            pltpu.VMEM((tiles, padded * rows, LANES), f32),
            pltpu.VMEM((2, plane, LANES), f32), pltpu.VMEM((padded * rows, LANES), f32),
            others, own, others, pltpu.VMEM((plane, cols - LANES), f32),
            pltpu.VMEM((2, plane, cols - LANES), f32), full, edges, edges, full, edges, edges, full, sides, full, full,
            pltpu.VMEM(qlon.shape, jnp.bfloat16),
            dma((2 + tiles,)), dma((2,)), dma((2,)), dma((n_lev - 1, 2 * chunks)), dma((n_lev - 1, 2 * chunks)),
            pair, pair, pair, pair, pair, pair, pair, pair, dma((chunks,)),
        ],
        compiler_params=pltpu.CompilerParams(
            collective_id=0, has_side_effects=True, vmem_limit_bytes=60 * 1024 * 1024
        ),
    )(
        gradient.reshape(plane, cols), vertical, variance.reshape(plane, cols),
        jnp.asarray(plat), jnp.asarray(qlon),
    )
    return result.reshape(levels, rows, cols)


def solution(mesh):
    return jax.shard_map(
        on_device,
        mesh=mesh,
        in_specs=(P("lev", "lat", "lon"), P(), P("lev", "lat", "lon")),
        out_specs=P("lev", "lat", "lon"),
        check_vma=False,
    )
```
